256 devices in a mesh: tok: 64 (over x, z, core), hid: 4 (over y).
Axes of the slice: x: 4, y: 4, z: 8, core: 2. Of those that a mesh axis runs over, the one named last changes fastest.
Arguments:
- activations: bfloat16 [131072, 8192], P('tok', 'hid'), may hold values from -6 to 6
- sketch: bfloat16 [8192, 320], P('hid'), may hold values from -0.0625 to 0.0625
Outputs:
- basis: float32 [131072, 320], P('tok')
- projected: float32 [8192, 320], P(('hid', 'tok'))
The draws below stay inside these ranges and needn't reach their ends.
All inputs are finite; a program needn't handle non-finite values.
Results may differ from the reference program's by a relative error of at most 0.00069.
Values sent between devices are 32-bit elements; how exact they have to be, the bound alone decides.
A program may use at most 128 MiB of HBM per device.

```python
import jax
import jax.numpy as jnp
from jax import lax

D = 8192
K = 320
TOKENS = 131072


def block_scale(key, shape, split, smallest, high):
    level = 1.0
    for axis_at, parts in split:
        heights = jax.random.uniform(jax.random.fold_in(jax.random.fold_in(key, 6), axis_at), (parts,), jnp.float32, smallest / len(split), high / len(split))
        level = level * jnp.repeat(jnp.exp(heights), shape[axis_at] // parts).reshape((-1,) + (1,) * (len(shape) - 1 - axis_at))
    return level


def normal_values(key, extent, spread, most, pieces=(), held_as=jnp.bfloat16):
    gain = block_scale(key, extent, pieces, -0.22, 0.18) if pieces else 1.0
    entries = jax.random.normal(key, extent, jnp.float32) * spread * gain
    return jnp.minimum(jnp.maximum(entries, -most), most).astype(held_as)


def setup_inputs(seed: int = 0) -> dict:
    streams_of = jax.random.split(jax.random.key(seed), 3)
    activations = normal_values(streams_of[0], (TOKENS, D), 1.0, 6.0, ((0, 64), (1, 4)))
    sketch = normal_values(streams_of[1], (D, K), D ** -0.5, 0.0625, ((0, 4),))
    return dict(activations=activations, sketch=sketch)


def reference(activations, sketch):
    sampled = jnp.dot(activations.astype(jnp.float32), sketch.astype(jnp.float32), preferred_element_type=jnp.float32)
    gram = jnp.dot(sampled.T.astype(jnp.float32), sampled.astype(jnp.float32), precision=lax.Precision.HIGHEST, preferred_element_type=jnp.float32)
    lower = jnp.linalg.cholesky(gram)
    basis = lax.linalg.triangular_solve(lower, sampled, left_side=False, lower=True, transpose_a=True)
    basis_bf = basis.astype(jnp.bfloat16)
    projected = lax.dot_general(activations.astype(jnp.float32), basis_bf.astype(jnp.float32), (((0,), (0,)), ((), ())), preferred_element_type=jnp.float32)
    return (basis, projected)
```

```python
import functools

import jax
import jax.numpy as jnp
from jax import lax
from jax.experimental import pallas as pl
from jax.experimental.pallas import tpu as pltpu
from jax.sharding import PartitionSpec as P

MESH = pl.DeviceIdType.MESH
HI = lax.Precision.HIGHEST
F32 = jnp.float32
BF = jnp.bfloat16
K = 320
B = 64
NP = 4
PR = K // NP


def rc(src, dst, ssem, rsem, dev):
    cp = pltpu.make_async_remote_copy(
        src_ref=src, dst_ref=dst, send_sem=ssem, recv_sem=rsem, device_id=dev, device_id_type=MESH
    )
    cp.start()
    return cp


def split(v):
    hi = v.astype(BF)
    return hi, (v - hi.astype(F32)).astype(BF)


def factor(aug):
    subl = lax.broadcasted_iota(jnp.int32, (8, 128), 0)
    parts = tuple(aug[8 * i : 8 * i + 8, :] for i in range(8))

    def panel(g, parts):
        top = parts[0]
        rest = [jnp.where(g + h < 8, parts[h], 0.0) for h in range(1, 8)]
        own = [jnp.broadcast_to(top[:, j : j + 1], (8, 128)) for j in range(8)]
        cols = [[jnp.broadcast_to(p[:, j : j + 1], (8, 128)) for j in range(8)] for p in rest]
        below = list(parts[1:])
        scale = jnp.zeros((8, 128), F32)
        for t in range(8):
            row = jnp.broadcast_to(top[t : t + 1, :], (8, 128))
            piv = jnp.broadcast_to(own[t][t : t + 1, :], (8, 128))
            inv = 1.0 / piv
            scale = jnp.where(subl == t, lax.rsqrt(piv), scale)
            f = jnp.where(subl > t, own[t] * inv, 0.0)
            later = [None] * 8
            for j in range(t + 1, 8):
                later[j] = jnp.broadcast_to(own[j][t : t + 1, :], (8, 128))
                own[j] = own[j] - f * later[j]
            top = top - f * row
            for h in range(7):
                fh = cols[h][t] * inv
                for j in range(t + 1, 8):
                    cols[h][j] = cols[h][j] - fh * later[j]
                below[h] = below[h] - fh * row
        top = top * scale
        return tuple(pltpu.roll(p, 120, 1) for p in below + [top])

    return jnp.concatenate(lax.fori_loop(0, 8, panel, parts), axis=0)


def chol_step(J, n_ref):
    r0 = B * J
    tile = 128 * (J // 2)
    blk = n_ref[r0 : r0 + B, tile : tile + 128]
    if J % 2:
        blk = pltpu.roll(blk, 64, 1)
    lanes = lax.broadcasted_iota(jnp.int32, (B, 128), 1)
    rows = lax.broadcasted_iota(jnp.int32, (B, 128), 0)
    w = factor(jnp.where(lanes < B, blk, (lanes - B == rows).astype(F32)))[:, :B]
    col = lax.broadcasted_iota(jnp.int32, (B, 384), 1)
    row = lax.broadcasted_iota(jnp.int32, (B, 384), 0)
    here = (col >= r0) & (col < r0 + B)
    rin = jnp.where(here, (row + r0 == col).astype(F32), n_ref[r0 : r0 + B, :])
    r = jnp.dot(w, rin, precision=HI, preferred_element_type=F32)
    n_ref[r0 : r0 + B, :] = jnp.where(col < r0 + B, r, 0.0)
    if J < K // B - 1:
        m = K - r0 - B
        upd = lax.dot_general(r, r, (((0,), (0,)), ((), ())), precision=HI, preferred_element_type=F32)
        colb = lax.broadcasted_iota(jnp.int32, (m, 384), 1)
        old = jnp.where((colb >= r0) & (colb < r0 + B), 0.0, n_ref[r0 + B : K, :])
        n_ref[r0 + B : K, :] = old - upd[r0 + B : K, :]


def main_kernel(
    a_hbm, s_ref, samp_out, linv_out, fin_out,
    a_v, own, rsr, samp, n_ref, pk, cr, g1, xr, zb, gf, shl, ct, crx, xs, xrr, zs, zr, fin,
    a_sem, rs_s, rs_r, ag_s, ag_r, fw_s, fw_r, core_s, core_r, xy_s, xy_r, z_s, z_r, xg_s, xg_r,
    px_s, px_r, pz_s, pz_r, out_sem,
):
    t = lax.axis_index("tok")
    y = lax.axis_index("hid")
    x, z, c = t // 16, (t // 2) % 8, t % 2

    def dev(dx=0, dy=0, dz=0, dc=0):
        xx, zz, cc = lax.rem(x + dx, 4), lax.rem(z + dz, 8), lax.rem(c + dc, 2)
        return (xx * 16 + zz * 2 + cc, lax.rem(y + dy, 4))

    sends = []

    def unit(i):
        k, d = i // 2, i % 2
        q = lax.rem(y + jnp.where(d == 0, 3 - k, 1 + k), 4)
        return q * 2 + d

    def a_copy(i):
        rows = pl.ds(pl.multiple_of(unit(i) * 256, 256), 256)
        return pltpu.make_async_copy(a_hbm.at[rows], a_v.at[rows], a_sem.at[i])

    for i in range(8):
        a_copy(i).start()

    barrier = pltpu.get_barrier_semaphore()
    xy = [(dx, dy) for dx in range(4) for dy in range(4) if dx + dy]
    peers = [dev(dx=dx, dy=dy) for dx, dy in xy] + [dev(dz=d) for d in range(1, 8)] + [dev(dc=1)]
    for p in peers:
        pl.semaphore_signal(barrier, inc=1, device_id=p, device_id_type=MESH)

    def work(i):
        a_copy(i).wait()
        rows = pl.ds(pl.multiple_of(unit(i) * 256, 256), 256)
        v = lax.dot_general(
            s_ref[...], a_v[rows, :], (((1,), (1,)), ((), ())), preferred_element_type=F32
        )
        own[i // 2, i % 2] = v.reshape(NP, PR, 256)

    ydir = [dev(dy=1), dev(dy=3)]
    work(0)
    work(1)
    pl.semaphore_wait(barrier, len(peers))
    for p in range(NP):
        for d in range(2):
            sends.append(rc(own.at[0, d, p], rsr.at[d, 0, p], rs_s.at[d, 0, p], rs_r.at[d, 0, p], ydir[d]))
    arrivals = {(0, d, p): sends[2 * p + d] for p in range(NP) for d in range(2)}

    @pl.loop(2, 8)
    def _(i):
        work(i)

    def ag_send(p):
        for d in range(2):
            cp = rc(samp.at[y, p], samp.at[y, p], ag_s.at[d, p], ag_r.at[d, p], ydir[d])
            sends.append(cp)
            arrivals["ag", d, p] = cp

    for s in range(3):
        for p in range(NP):
            for d in range(2):
                arrivals[s, d, p].wait_recv()
                v = rsr[d, s, p] + own[s + 1, d, p]
                if s < 2:
                    rsr[d, s, p] = v
                    cp = rc(
                        rsr.at[d, s, p], rsr.at[d, s + 1, p], rs_s.at[d, s + 1, p], rs_r.at[d, s + 1, p], ydir[d]
                    )
                    sends.append(cp)
                    arrivals[s + 1, d, p] = cp
                else:
                    samp[y, p, d] = v
            if s == 2 and p < 2:
                ag_send(p)

    def ag_forward(p):
        for d in range(2):
            arrivals["ag", d, p].wait_recv()
            q = lax.rem(y + (3 if d == 0 else 1), 4)
            cp = rc(samp.at[q, p, d], samp.at[q, p, d], fw_s.at[d, p], fw_r.at[d, p], ydir[d])
            sends.append(cp)
            arrivals["fw", d, p] = cp

    gram = jnp.zeros((K, K), F32)
    for d in range(2):
        v = samp[y, :, d].reshape(K, 256)
        gram = gram + lax.dot_general(v, v, (((1,), (1,)), ((), ())), precision=HI, preferred_element_type=F32)
    n_ref[...] = jnp.zeros_like(n_ref)
    n_ref[:, 0:K] = gram
    low = lax.broadcasted_iota(jnp.int32, (B, 128), 1) < B

    def tile(i, j):
        return n_ref[B * i : B * i + B, 128 * j : 128 * j + 128]

    panels = [
        tile(0, 0),
        tile(0, 1),
        tile(1, 1),
        tile(2, 1),
        jnp.where(low, tile(0, 2), tile(1, 0)),
        jnp.where(low, tile(1, 2), tile(3, 1)),
        jnp.where(low, tile(2, 2), pltpu.roll(tile(3, 2), 64, 1)),
        tile(4, 2),
    ]
    for i, v in enumerate(panels):
        pk[i // 4, 4 * (i % 4) : 4 * (i % 4) + 4] = v.reshape(4, 16, 128)

    other = dev(dc=1)
    cp = rc(pk.at[1 - c], cr, core_s.at[0], core_r.at[0], other)
    sends.append(cp)
    cp.wait_recv()
    g1[...] = pk[c] + cr[...]
    me = 4 * x + y
    cps = []
    for i, (dx, dy) in enumerate(xy):
        to = 4 * lax.rem(x + dx, 4) + lax.rem(y + dy, 4)
        cps.append(rc(g1.at[to], xr.at[i], xy_s.at[i], xy_r.at[i], dev(dx=dx, dy=dy)))
    ag_send(2)
    ag_send(3)
    ag_forward(0)
    ag_forward(1)
    v = g1[me]
    for i, cp in enumerate(cps):
        cp.wait_recv()
        v = v + xr[i]
    sends += cps
    zb[z] = v
    cps = [rc(zb.at[z], zb.at[z], z_s.at[d - 1], z_r.at[d - 1], dev(dz=d)) for d in range(1, 8)]
    for cp in cps:
        cp.wait_recv()
    sends += cps
    v = zb[0]
    for i in range(1, 8):
        v = v + zb[i]
    gf[c, me] = v
    cps = [
        rc(gf.at[c, me], gf.at[c, me], xg_s.at[i], xg_r.at[i], dev(dx=dx, dy=dy)) for i, (dx, dy) in enumerate(xy)
    ]
    for cp in cps:
        cp.wait_recv()
    sends += cps
    cp = rc(gf.at[c], gf.at[c], core_s.at[1], core_r.at[1], other)
    sends.append(cp)
    cp.wait_recv()

    def panel(i):
        return gf[i // 4, 4 * (i % 4) : 4 * (i % 4) + 4].reshape(B, 128)

    def put(i, j, v):
        n_ref[B * i : B * i + B, 128 * j : 128 * j + 128] = v

    put(0, 0, panel(0))
    put(0, 1, panel(1))
    put(1, 1, panel(2))
    put(2, 1, panel(3))
    v = panel(4)
    put(0, 2, jnp.where(low, v, 0.0))
    put(1, 0, jnp.where(low, 0.0, v))
    v = panel(5)
    put(1, 2, jnp.where(low, v, 0.0))
    put(3, 1, jnp.where(low, 0.0, v))
    v = panel(6)
    put(2, 2, jnp.where(low, v, 0.0))
    put(3, 2, jnp.where(low, pltpu.roll(v, 64, 1), 0.0))
    put(4, 2, panel(7))

    def c_work(h):
        for u in range(8):
            hi, lo = split(samp[u // 2, 2 * h : 2 * h + 2, u % 2].reshape(2 * PR, 256))
            shl[0 : 2 * PR, 256 * u : 256 * u + 256] = hi
            shl[2 * PR : 4 * PR, 256 * u : 256 * u + 256] = lo

        @pl.loop(0, 8)
        def _(j):
            cols = pl.ds(pl.multiple_of(256 * j, 256), 256)
            v = jnp.dot(shl[...], a_v[:, cols], preferred_element_type=F32)
            ct[h, :, :, cols] = (v[0 : 2 * PR] + v[2 * PR : 4 * PR]).reshape(2, PR, 256)

        cp = rc(ct.at[h, 1 - c], crx.at[h], core_s.at[2 + h], core_r.at[2 + h], other)
        sends.append(cp)
        arrivals["c", h] = cp

    def x_start(h):
        arrivals["c", h].wait_recv()
        for i in range(4):
            xs[h, i] = ct[h, c, :, 512 * i : 512 * i + 512] + crx[h, :, 512 * i : 512 * i + 512]
        arrivals["x", h] = [
            rc(xs.at[h, lax.rem(x + d, 4)], xrr.at[h, d - 1], px_s.at[h, d - 1], px_r.at[h, d - 1], dev(dx=d))
            for d in range(1, 4)
        ]
        sends.extend(arrivals["x", h])

    def z_start(h):
        for cp in arrivals["x", h]:
            cp.wait_recv()
        v = xs[h, x] + xrr[h, 0] + xrr[h, 1] + xrr[h, 2]
        half = lax.broadcasted_iota(jnp.int32, (PR // 2, 128), 1) < 64
        for i in range(8):
            w = v[:, 128 * (i // 2) : 128 * (i // 2) + 128]
            top, bottom = w[0 : PR // 2], w[PR // 2 : PR]
            if i % 2:
                zs[h, i] = jnp.where(half, pltpu.roll(top, 64, 1), bottom)
            else:
                zs[h, i] = jnp.where(half, top, pltpu.roll(bottom, 64, 1))
        arrivals["z", h] = [
            rc(zs.at[h, lax.rem(z + d, 8)], zr.at[h, d - 1], pz_s.at[h, d - 1], pz_r.at[h, d - 1], dev(dz=d))
            for d in range(1, 8)
        ]
        sends.extend(arrivals["z", h])

    def z_end(h):
        v = zs[h, z]
        for i, cp in enumerate(arrivals["z", h]):
            cp.wait_recv()
            v = v + zr[h, i]
        fin[h, c] = v
        cp = rc(fin.at[h, c], fin.at[h, c], core_s.at[4 + h], core_r.at[4 + h], other)
        sends.append(cp)
        arrivals["fin", h] = cp

    def ag_end(p):
        for d in range(2):
            arrivals["fw", d, p].wait_recv()

    chol_step(0, n_ref)
    ag_forward(2)
    ag_forward(3)
    ag_end(0)
    ag_end(1)
    c_work(0)
    chol_step(1, n_ref)
    x_start(0)
    chol_step(2, n_ref)
    ag_end(2)
    ag_end(3)
    out = pltpu.make_async_copy(samp, samp_out, out_sem.at[0])
    out.start()
    c_work(1)
    x_start(1)
    z_start(0)
    chol_step(3, n_ref)
    z_end(0)
    z_start(1)
    chol_step(4, n_ref)
    linv_out[...] = n_ref[...]
    z_end(1)
    for h in range(2):
        arrivals["fin", h].wait_recv()
    out.wait()
    fin_out[...] = fin[...]
    for cp in sends:
        cp.wait_send()


def last_kernel(core, samp_ref, linv_ref, fin_ref, basis_ref, proj_ref):
    whi, wlo = split(linv_ref[:, 0:K])

    def times(v):
        hi, lo = split(v)
        dot = functools.partial(jnp.dot, preferred_element_type=F32)
        return dot(whi, hi) + (dot(whi, lo) + dot(wlo, hi))

    basis_ref[...] = times(samp_ref[0, :, 0].reshape(K, 256))

    @pl.when(pl.program_id(0) == 0)
    def _():
        rows = []
        for p in range(NP):
            v = fin_ref[p // 2, p % 2]
            rows += [v, pltpu.roll(v, 64, 1)]
        v = jnp.transpose(times(jnp.concatenate(rows, axis=0)))
        proj_ref[...] = jnp.where(core[0] == 0, v[0:32], v[32:64])


def local(activations, sketch):
    dma = pltpu.SemaphoreType.DMA
    vm = pltpu.VMEM
    samp, linv, fin = pl.pallas_call(
        main_kernel,
        out_shape=(
            jax.ShapeDtypeStruct((4, NP, 2, PR, 256), F32),
            jax.ShapeDtypeStruct((K, 384), F32),
            jax.ShapeDtypeStruct((2, 2, PR // 2, 128), F32),
        ),
        in_specs=[pl.BlockSpec(memory_space=pl.ANY), pl.BlockSpec(memory_space=vm)],
        out_specs=(
            pl.BlockSpec(memory_space=pl.ANY),
            pl.BlockSpec(memory_space=vm),
            pl.BlockSpec(memory_space=vm),
        ),
        scratch_shapes=[
            vm((2048, 2048), BF),
            vm((4, 2, NP, PR, 256), F32),
            vm((2, 3, NP, PR, 256), F32),
            vm((4, NP, 2, PR, 256), F32),
            vm((K, 384), F32),
            vm((2, 16, 16, 128), F32),
            vm((16, 16, 128), F32),
            vm((16, 16, 128), F32),
            vm((15, 16, 128), F32),
            vm((8, 16, 128), F32),
            vm((2, 16, 16, 128), F32),
            vm((4 * PR, 2048), BF),
            vm((2, 2, PR, 2048), F32),
            vm((2, PR, 2048), F32),
            vm((2, 4, PR, 512), F32),
            vm((2, 3, PR, 512), F32),
            vm((2, 8, PR // 2, 128), F32),
            vm((2, 7, PR // 2, 128), F32),
            vm((2, 2, PR // 2, 128), F32),
            dma((8,)),
            dma((2, 3, NP)),
            dma((2, 3, NP)),
            dma((2, NP)),
            dma((2, NP)),
            dma((2, NP)),
            dma((2, NP)),
            dma((6,)),
            dma((6,)),
            dma((15,)),
            dma((15,)),
            dma((7,)),
            dma((7,)),
            dma((15,)),
            dma((15,)),
            dma((2, 3)),
            dma((2, 3)),
            dma((2, 7)),
            dma((2, 7)),
            dma((1,)),
        ],
        compiler_params=pltpu.CompilerParams(
            collective_id=0, has_side_effects=True, vmem_limit_bytes=56 * 1024 * 1024
        ),
        name="main",
    )(activations, sketch.T)
    core = (lax.axis_index("tok") % 2).astype(jnp.int32).reshape(1)
    basis, proj = pl.pallas_call(
        last_kernel,
        grid_spec=pltpu.PrefetchScalarGridSpec(
            num_scalar_prefetch=1,
            grid=(8,),
            in_specs=[
                pl.BlockSpec((1, NP, 1, PR, 256), lambda i, core: (i // 2, 0, i % 2, 0, 0)),
                pl.BlockSpec((K, 384), lambda i, core: (0, 0)),
                pl.BlockSpec((2, 2, PR // 2, 128), lambda i, core: (0, 0, 0, 0)),
            ],
            out_specs=[
                pl.BlockSpec((K, 256), lambda i, core: (0, i)),
                pl.BlockSpec((32, K), lambda i, core: (0, 0)),
            ],
        ),
        out_shape=(jax.ShapeDtypeStruct((K, 2048), F32), jax.ShapeDtypeStruct((32, K), F32)),
        compiler_params=pltpu.CompilerParams(vmem_limit_bytes=32 * 1024 * 1024),
        name="last",
    )(core, samp, linv, fin)
    return basis.T, proj


def solution(mesh):
    in_specs = (P("tok", "hid"), P("hid", None))
    out_specs = (P("tok", None), P(("hid", "tok"), None))
    return jax.shard_map(local, mesh=mesh, in_specs=in_specs, out_specs=out_specs, check_vma=False)
```

```python
import functools

import jax
import jax.numpy as jnp
from jax import lax
from jax.experimental import pallas as pl
from jax.experimental.pallas import tpu as pltpu
from jax.sharding import PartitionSpec as P

MESH = pl.DeviceIdType.MESH
HI = lax.Precision.HIGHEST
F32 = jnp.float32
BF = jnp.bfloat16
K = 320
B = 64
NP = 5
PR = K // NP
GROUPS = ((0, 2), (2, 4), (4, 5))
SIZES = tuple((b - a) * PR // 2 for a, b in GROUPS)


def rc(src, dst, ssem, rsem, dev):
    cp = pltpu.make_async_remote_copy(
        src_ref=src, dst_ref=dst, send_sem=ssem, recv_sem=rsem, device_id=dev, device_id_type=MESH
    )
    cp.start()
    return cp


def split(v):
    hi = v.astype(BF)
    return hi, (v - hi.astype(F32)).astype(BF)


def factor(aug):
    subl = lax.broadcasted_iota(jnp.int32, (8, 128), 0)
    w = 16
    n = w // 8

    def spread(v, i):
        return jnp.broadcast_to(v[i : i + 1, :], (8, 128))

    parts = [aug[8 * i : 8 * i + 8, :] for i in range(8)]
    for g in range(0, 8, n):
        cur = parts[g:]
        cols = [[jnp.broadcast_to(v[:, 8 * g + j : 8 * g + j + 1], (8, 128)) for j in range(w)] for v in cur]
        scale = [jnp.zeros((8, 128), F32) for _ in range(n)]
        for t in range(w):
            o, i = t // 8, t % 8
            piv = spread(cols[o][t], i)
            inv = 1.0 / piv
            scale[o] = jnp.where(subl == i, lax.rsqrt(piv), scale[o])
            row = spread(cur[o], i)
            later = {j: spread(cols[o][j], i) for j in range(t + 1, w)}
            for h in range(o, len(cur)):
                f = cols[h][t] * inv
                if h == o:
                    f = jnp.where(subl > i, f, 0.0)
                for j in range(t + 1, w):
                    cols[h][j] = cols[h][j] - f * later[j]
                cur[h] = cur[h] - f * row
        parts = parts[:g] + [cur[o] * scale[o] for o in range(n)] + cur[n:]
    return jnp.concatenate(parts, axis=0)


def chol_step(J, n_ref):
    r0 = B * J
    tile = 128 * (J // 2)
    blk = n_ref[r0 : r0 + B, tile : tile + 128]
    if J % 2:
        blk = pltpu.roll(blk, 64, 1)
    lanes = lax.broadcasted_iota(jnp.int32, (B, 128), 1)
    rows = lax.broadcasted_iota(jnp.int32, (B, 128), 0)
    w = pltpu.roll(factor(jnp.where(lanes < B, blk, (lanes - B == rows).astype(F32))), 64, 1)[:, :B]
    col = lax.broadcasted_iota(jnp.int32, (B, 384), 1)
    row = lax.broadcasted_iota(jnp.int32, (B, 384), 0)
    here = (col >= r0) & (col < r0 + B)
    rin = jnp.where(here, (row + r0 == col).astype(F32), n_ref[r0 : r0 + B, :])
    r = jnp.dot(w, rin, precision=HI, preferred_element_type=F32)
    n_ref[r0 : r0 + B, :] = jnp.where(col < r0 + B, r, 0.0)
    if J < K // B - 1:
        m = K - r0 - B
        upd = lax.dot_general(r, r, (((0,), (0,)), ((), ())), precision=HI, preferred_element_type=F32)
        colb = lax.broadcasted_iota(jnp.int32, (m, 384), 1)
        old = jnp.where((colb >= r0) & (colb < r0 + B), 0.0, n_ref[r0 + B : K, :])
        n_ref[r0 + B : K, :] = old - upd[r0 + B : K, :]


def main_kernel(
    a_hbm, s_hbm, bs, proj_out,
    a_v, s_ref, own, rsr, samp, n_ref, pk, cr, g1, xr, zb, gf, shl,
    ct0, ct1, ct2, crx0, crx1, crx2, xs0, xs1, xs2, xrr0, xrr1, xrr2, zs0, zs1, zs2, zr0, zr1, zr2,
    fin0, fin1, fin2,
    a_sem, rs_s, rs_r, ag_s, ag_r, fw_s, fw_r, core_s, core_r, xy_s, xy_r, z_s, z_r, xg_s, xg_r,
    px_s, px_r, pz_s, pz_r,
):
    ct, crx, xs, xrr = (ct0, ct1, ct2), (crx0, crx1, crx2), (xs0, xs1, xs2), (xrr0, xrr1, xrr2)
    zs, zr, fin = (zs0, zs1, zs2), (zr0, zr1, zr2), (fin0, fin1, fin2)
    t = lax.axis_index("tok")
    y = lax.axis_index("hid")
    x, z, c = t // 16, (t // 2) % 8, t % 2

    def dev(dx=0, dy=0, dz=0, dc=0):
        xx, zz, cc = lax.rem(x + dx, 4), lax.rem(z + dz, 8), lax.rem(c + dc, 2)
        return (xx * 16 + zz * 2 + cc, lax.rem(y + dy, 4))

    sends = []

    def unit(i):
        k, d = i // 2, i % 2
        q = lax.rem(y + jnp.where(d == 0, 3 - k, 1 + k), 4)
        return q * 2 + d

    def a_copy(i):
        rows = pl.ds(pl.multiple_of(unit(i) * 256, 256), 256)
        return pltpu.make_async_copy(a_hbm.at[rows], a_v.at[rows], a_sem.at[i])

    barrier = pltpu.get_barrier_semaphore()
    xy = [(dx, dy) for dx in range(4) for dy in range(4) if dx + dy]
    peers = [dev(dy=1), dev(dy=3), dev(dc=1)] + [dev(dz=d) for d in range(1, 8)]
    peers += [dev(dx=dx, dy=dy) for dx, dy in xy if (dx, dy) not in ((0, 1), (0, 3))]
    for p in peers:
        pl.semaphore_signal(barrier, inc=1, device_id=p, device_id_type=MESH)
    s_copy = pltpu.make_async_copy(s_hbm, s_ref, a_sem.at[8])
    s_copy.start()
    a_copy(0).start()
    a_copy(1).start()
    s_copy.wait()

    def work(i, ahead=()):
        a_copy(i).wait()
        for j in ahead:
            a_copy(j).start()
        rows = pl.ds(pl.multiple_of(unit(i) * 256, 256), 256)
        v = lax.dot_general(
            s_ref[...], a_v[rows, :], (((1,), (1,)), ((), ())), preferred_element_type=F32
        )
        own[i // 2, i % 2] = v.reshape(NP, PR, 256)

    ydir = [dev(dy=1), dev(dy=3)]
    work(0, range(2, 4))
    work(1, range(4, 8))
    pl.semaphore_wait(barrier, len(peers))
    for p in range(NP):
        for d in range(2):
            sends.append(rc(own.at[0, d, p], rsr.at[d, 0, p], rs_s.at[d, 0, p], rs_r.at[d, 0, p], ydir[d]))
    arrivals = {(0, d, p): sends[2 * p + d] for p in range(NP) for d in range(2)}

    @pl.loop(2, 8)
    def _(i):
        work(i)

    def ag_send(p):
        for d in range(2):
            cp = rc(samp.at[y, p], samp.at[y, p], ag_s.at[d, p], ag_r.at[d, p], ydir[d])
            sends.append(cp)
            arrivals["ag", d, p] = cp

    def gram(p):
        v = None
        for d in range(2):
            u = lax.dot_general(
                samp[y, 0 : p + 1, d].reshape((p + 1) * PR, 256),
                samp[y, p, d],
                (((1,), (1,)), ((), ())),
                precision=HI,
                preferred_element_type=F32,
            )
            v = u if v is None else v + u
        n_ref[0 : (p + 1) * PR, p * PR : (p + 1) * PR] = v

    n_ref[...] = jnp.zeros_like(n_ref)
    for s in range(3):
        for p in range(NP):
            for d in range(2):
                arrivals[s, d, p].wait_recv()
                v = rsr[d, s, p] + own[s + 1, d, p]
                if s < 2:
                    rsr[d, s, p] = v
                    cp = rc(
                        rsr.at[d, s, p], rsr.at[d, s + 1, p], rs_s.at[d, s + 1, p], rs_r.at[d, s + 1, p], ydir[d]
                    )
                    sends.append(cp)
                    arrivals[s + 1, d, p] = cp
                else:
                    samp[y, p, d] = v
            if s == 2:
                if p < 3:
                    ag_send(p)
                gram(p)

    def ag_forward(p):
        for d in range(2):
            arrivals["ag", d, p].wait_recv()
            q = lax.rem(y + (3 if d == 0 else 1), 4)
            cp = rc(samp.at[q, p, d], samp.at[q, p, d], fw_s.at[d, p], fw_r.at[d, p], ydir[d])
            sends.append(cp)
            arrivals["fw", d, p] = cp

    def ag_end(p):
        for d in range(2):
            arrivals["fw", d, p].wait_recv()

    ring = (0, 1, 3, 2)

    def c_part(h, steps, first):
        a, b = GROUPS[h]
        r = 2 * SIZES[h]
        for i in steps:
            q = lax.rem(y + ring[i], 4)
            for d in range(2):
                hi, lo = split(samp[q, a:b, d].reshape(r, 256))
                shl[i, 0:r, 256 * d : 256 * d + 256] = hi
                shl[i, r : 2 * r, 256 * d : 256 * d + 256] = lo

        @pl.loop(0, 4)
        def _(j):
            cols = pl.ds(pl.multiple_of(512 * j, 512), 512)
            v = None
            for i in steps:
                rows = pl.ds(pl.multiple_of(512 * lax.rem(y + ring[i], 4), 512), 512)
                u = jnp.dot(shl[i, 0 : 2 * r], a_v[rows, cols], preferred_element_type=F32)
                v = u if v is None else v + u
            v = (v[0:r] + v[r : 2 * r]).reshape(2, r // 2, 512)
            ct[h][:, :, cols] = v if first else ct[h][:, :, cols] + v

    def c_send(h):
        cp = rc(ct[h].at[1 - c], crx[h], core_s.at[2 + h], core_r.at[2 + h], dev(dc=1))
        sends.append(cp)
        arrivals["c", h] = cp

    def c_work(h):
        c_part(h, range(4), True)
        c_send(h)

    def x_start(h):
        arrivals["c", h].wait_recv()
        for i in range(4):
            xs[h][i] = ct[h][c, :, 512 * i : 512 * i + 512] + crx[h][:, 512 * i : 512 * i + 512]
        arrivals["x", h] = [
            rc(xs[h].at[lax.rem(x + d, 4)], xrr[h].at[d - 1], px_s.at[h, d - 1], px_r.at[h, d - 1], dev(dx=d))
            for d in range(1, 4)
        ]
        sends.extend(arrivals["x", h])

    def z_start(h):
        for cp in arrivals["x", h]:
            cp.wait_recv()
        v = xs[h][x] + xrr[h][0] + xrr[h][1] + xrr[h][2]
        n = SIZES[h] // 2
        half = lax.broadcasted_iota(jnp.int32, (n, 128), 1) < 64
        for i in range(8):
            w = v[:, 128 * (i // 2) : 128 * (i // 2) + 128]
            top, bottom = w[0:n], w[n : 2 * n]
            if i % 2:
                zs[h][i] = jnp.where(half, pltpu.roll(top, 64, 1), bottom)
            else:
                zs[h][i] = jnp.where(half, top, pltpu.roll(bottom, 64, 1))
        arrivals["z", h] = [
            rc(zs[h].at[lax.rem(z + d, 8)], zr[h].at[d - 1], pz_s.at[h, d - 1], pz_r.at[h, d - 1], dev(dz=d))
            for d in range(1, 8)
        ]
        sends.extend(arrivals["z", h])

    def z_end(h):
        v = zs[h][z]
        for i, cp in enumerate(arrivals["z", h]):
            cp.wait_recv()
            v = v + zr[h][i]
        fin[h][c] = v
        cp = rc(fin[h].at[c], fin[h].at[c], core_s.at[5 + h], core_r.at[5 + h], dev(dc=1))
        sends.append(cp)
        arrivals["fin", h] = cp

    dot = functools.partial(jnp.dot, preferred_element_type=F32)

    def basis():
        whi, wlo = split(n_ref[:, 0:K])
        both = jnp.concatenate([whi[0:256, 0:256], wlo[0:256, 0:256]], axis=0)
        low = jnp.concatenate([whi[256:K], wlo[256:K]], axis=0)

        @pl.loop(0, 8)
        def _(u):
            hi, lo = split(samp[u // 2, :, u % 2].reshape(K, 256))
            cols = pl.ds(pl.multiple_of(256 * u, 256), 256)
            v = dot(both, hi[0:256])
            bs[0:256, cols] = v[0:256] + (v[256:512] + dot(whi[0:256, 0:256], lo[0:256]))
            v = dot(low, hi)
            bs[256:K, cols] = v[0:64] + (v[64:128] + dot(whi[256:K], lo))

    def projected():
        for h in range(len(GROUPS)):
            arrivals["fin", h].wait_recv()
        rows = []
        for h in range(len(GROUPS)):
            for i in range(2):
                rows += [fin[h][i], pltpu.roll(fin[h][i], 64, 1)]
        v = jnp.dot(n_ref[:, 0:K], jnp.concatenate(rows, axis=0), precision=HI, preferred_element_type=F32)
        v = jnp.transpose(v)
        proj_out[...] = jnp.where(c == 0, v[0:32], v[32:64])

    low = lax.broadcasted_iota(jnp.int32, (B, 128), 1) < B

    def tile(i, j):
        return n_ref[B * i : B * i + B, 128 * j : 128 * j + 128]

    panels = [
        tile(0, 0),
        tile(0, 1),
        tile(1, 1),
        tile(2, 1),
        jnp.where(low, tile(0, 2), tile(1, 0)),
        jnp.where(low, tile(1, 2), tile(3, 1)),
        jnp.where(low, tile(2, 2), pltpu.roll(tile(3, 2), 64, 1)),
        tile(4, 2),
    ]
    for i, v in enumerate(panels):
        pk[i // 4, 4 * (i % 4) : 4 * (i % 4) + 4] = v.reshape(4, 16, 128)

    other = dev(dc=1)
    cp = rc(pk.at[1 - c], cr, core_s.at[0], core_r.at[0], other)
    sends.append(cp)
    cp.wait_recv()
    g1[...] = pk[c] + cr[...]
    me = 4 * x + y
    cps = []
    for i, (dx, dy) in enumerate(xy):
        to = 4 * lax.rem(x + dx, 4) + lax.rem(y + dy, 4)
        cps.append(rc(g1.at[to], xr.at[i], xy_s.at[i], xy_r.at[i], dev(dx=dx, dy=dy)))
    ag_forward(0)
    ag_send(3)
    v = g1[me]
    for i, cp in enumerate(cps):
        cp.wait_recv()
        v = v + xr[i]
    sends += cps
    zb[z] = v
    cps = [rc(zb.at[z], zb.at[z], z_s.at[d - 1], z_r.at[d - 1], dev(dz=d)) for d in range(1, 8)]
    ag_forward(1)
    ag_send(4)
    for cp in cps:
        cp.wait_recv()
    sends += cps
    v = zb[0]
    for i in range(1, 8):
        v = v + zb[i]
    gf[c, me] = v
    cps = [
        rc(gf.at[c, me], gf.at[c, me], xg_s.at[i], xg_r.at[i], dev(dx=dx, dy=dy)) for i, (dx, dy) in enumerate(xy)
    ]
    sends += cps
    ag_forward(2)
    ag_forward(3)
    ag_end(0)
    ag_end(1)
    c_work(0)
    for cp in cps:
        cp.wait_recv()
    cp = rc(gf.at[c], gf.at[c], core_s.at[1], core_r.at[1], other)
    sends.append(cp)
    ag_forward(4)
    cp.wait_recv()

    def panel(i):
        return gf[i // 4, 4 * (i % 4) : 4 * (i % 4) + 4].reshape(B, 128)

    def put(i, j, v):
        n_ref[B * i : B * i + B, 128 * j : 128 * j + 128] = v

    put(0, 0, panel(0))
    put(0, 1, panel(1))
    put(1, 1, panel(2))
    put(2, 1, panel(3))
    v = panel(4)
    put(0, 2, jnp.where(low, v, 0.0))
    put(1, 0, jnp.where(low, 0.0, v))
    v = panel(5)
    put(1, 2, jnp.where(low, v, 0.0))
    put(3, 1, jnp.where(low, 0.0, v))
    v = panel(6)
    put(2, 2, jnp.where(low, v, 0.0))
    put(3, 2, jnp.where(low, pltpu.roll(v, 64, 1), 0.0))
    put(4, 2, panel(7))

    x_start(0)
    ag_end(2)
    ag_end(3)
    c_work(1)
    ag_end(4)
    c_work(2)
    x_start(1)
    z_start(0)
    chol_step(0, n_ref)
    x_start(2)
    chol_step(1, n_ref)
    z_end(0)
    z_start(1)
    chol_step(2, n_ref)
    z_start(2)
    chol_step(3, n_ref)
    z_end(1)
    chol_step(4, n_ref)
    z_end(2)
    basis()
    projected()
    for cp in sends:
        cp.wait_send()


def local(activations, sketch):
    dma = pltpu.SemaphoreType.DMA
    vm = pltpu.VMEM
    n = len(GROUPS)
    basis, proj = pl.pallas_call(
        main_kernel,
        out_shape=(vm((K, 2048), F32), vm((32, K), F32)),
        in_specs=[pl.BlockSpec(memory_space=pl.ANY)] * 2,
        out_specs=(pl.BlockSpec(memory_space=vm), pl.BlockSpec(memory_space=vm)),
        scratch_shapes=[
            vm((2048, 2048), BF),
            vm((K, 2048), BF),
            vm((4, 2, NP, PR, 256), F32),
            vm((2, 3, NP, PR, 256), F32),
            vm((4, NP, 2, PR, 256), F32),
            vm((K, 384), F32),
            vm((2, 16, 16, 128), F32),
            vm((16, 16, 128), F32),
            vm((16, 16, 128), F32),
            vm((15, 16, 128), F32),
            vm((8, 16, 128), F32),
            vm((2, 16, 16, 128), F32),
            vm((4, 4 * max(SIZES), 512), BF),
            *[vm((2, r, 2048), F32) for r in SIZES],
            *[vm((r, 2048), F32) for r in SIZES],
            *[vm((4, r, 512), F32) for r in SIZES],
            *[vm((3, r, 512), F32) for r in SIZES],
            *[vm((8, r // 2, 128), F32) for r in SIZES],
            *[vm((7, r // 2, 128), F32) for r in SIZES],
            *[vm((2, r // 2, 128), F32) for r in SIZES],
            dma((9,)),
            dma((2, 3, NP)),
            dma((2, 3, NP)),
            dma((2, NP)),
            dma((2, NP)),
            dma((2, NP)),
            dma((2, NP)),
            dma((2 + 2 * n,)),
            dma((2 + 2 * n,)),
            dma((15,)),
            dma((15,)),
            dma((7,)),
            dma((7,)),
            dma((15,)),
            dma((15,)),
            dma((n, 3)),
            dma((n, 3)),
            dma((n, 7)),
            dma((n, 7)),
        ],
        compiler_params=pltpu.CompilerParams(
            collective_id=0, has_side_effects=True, vmem_limit_bytes=58 * 1024 * 1024
        ),
        name="main",
    )(activations, sketch.T)
    return basis.T, proj


def solution(mesh):
    in_specs = (P("tok", "hid"), P("hid", None))
    out_specs = (P("tok", None), P(("hid", "tok"), None))
    return jax.shard_map(local, mesh=mesh, in_specs=in_specs, out_specs=out_specs, check_vma=False)
```

```python
import functools

import jax
import jax.numpy as jnp
from jax import lax
from jax.experimental import pallas as pl
from jax.experimental.pallas import tpu as pltpu
from jax.sharding import PartitionSpec as P

MESH = pl.DeviceIdType.MESH
HI = lax.Precision.HIGHEST
F32 = jnp.float32
BF = jnp.bfloat16
K = 320
B = 64
NP = 5
PR = K // NP
GROUPS = ((0, 3), (3, 5))
SIZES = tuple((b - a) * PR // 2 for a, b in GROUPS)


def rc(src, dst, ssem, rsem, dev):
    cp = pltpu.make_async_remote_copy(
        src_ref=src, dst_ref=dst, send_sem=ssem, recv_sem=rsem, device_id=dev, device_id_type=MESH
    )
    cp.start()
    return cp


def split(v):
    hi = v.astype(BF)
    return hi, (v - hi.astype(F32)).astype(BF)


def factor(aug):
    subl = lax.broadcasted_iota(jnp.int32, (8, 128), 0)
    w = 16
    n = w // 8

    def spread(v, i):
        return jnp.broadcast_to(v[i : i + 1, :], (8, 128))

    parts = [aug[8 * i : 8 * i + 8, :] for i in range(8)]
    for g in range(0, 8, n):
        cur = parts[g:]
        cols = [[jnp.broadcast_to(v[:, 8 * g + j : 8 * g + j + 1], (8, 128)) for j in range(w)] for v in cur]
        scale = [jnp.zeros((8, 128), F32) for _ in range(n)]
        for t in range(w):
            o, i = t // 8, t % 8
            piv = spread(cols[o][t], i)
            inv = 1.0 / piv
            scale[o] = jnp.where(subl == i, lax.rsqrt(piv), scale[o])
            row = spread(cur[o], i)
            later = {j: spread(cols[o][j], i) for j in range(t + 1, w)}
            for h in range(o, len(cur)):
                f = cols[h][t] * inv
                if h == o:
                    f = jnp.where(subl > i, f, 0.0)
                for j in range(t + 1, w):
                    cols[h][j] = cols[h][j] - f * later[j]
                cur[h] = cur[h] - f * row
        parts = parts[:g] + [cur[o] * scale[o] for o in range(n)] + cur[n:]
    return jnp.concatenate(parts, axis=0)


def chol_step(J, n_ref):
    r0 = B * J
    tile = 128 * (J // 2)
    blk = n_ref[r0 : r0 + B, tile : tile + 128]
    if J % 2:
        blk = pltpu.roll(blk, 64, 1)
    lanes = lax.broadcasted_iota(jnp.int32, (B, 128), 1)
    rows = lax.broadcasted_iota(jnp.int32, (B, 128), 0)
    w = pltpu.roll(factor(jnp.where(lanes < B, blk, (lanes - B == rows).astype(F32))), 64, 1)[:, :B]
    col = lax.broadcasted_iota(jnp.int32, (B, 384), 1)
    row = lax.broadcasted_iota(jnp.int32, (B, 384), 0)
    here = (col >= r0) & (col < r0 + B)
    rin = jnp.where(here, (row + r0 == col).astype(F32), n_ref[r0 : r0 + B, :])
    r = jnp.dot(w, rin, precision=HI, preferred_element_type=F32)
    n_ref[r0 : r0 + B, :] = jnp.where(col < r0 + B, r, 0.0)
    if J < K // B - 1:
        m = K - r0 - B
        upd = lax.dot_general(r, r, (((0,), (0,)), ((), ())), precision=HI, preferred_element_type=F32)
        colb = lax.broadcasted_iota(jnp.int32, (m, 384), 1)
        old = jnp.where((colb >= r0) & (colb < r0 + B), 0.0, n_ref[r0 + B : K, :])
        n_ref[r0 + B : K, :] = old - upd[r0 + B : K, :]


def main_kernel(
    a_hbm, s_hbm, bs, proj_out,
    a_v, s_ref, own, rsr, samp, n_ref, pk, cr, g1, xr, zb, gf, shl,
    ct0, ct1, crx0, crx1, xs0, xs1, xrr0, xrr1, zs0, zs1, zr0, zr1, fin0, fin1,
    a_sem, rs_s, rs_r, ag_s, ag_r, fw_s, fw_r, core_s, core_r, xy_s, xy_r, z_s, z_r, xg_s, xg_r,
    px_s, px_r, pz_s, pz_r,
):
    ct, crx, xs, xrr = (ct0, ct1), (crx0, crx1), (xs0, xs1), (xrr0, xrr1)
    zs, zr, fin = (zs0, zs1), (zr0, zr1), (fin0, fin1)
    t = lax.axis_index("tok")
    y = lax.axis_index("hid")
    x, z, c = t // 16, (t // 2) % 8, t % 2

    def dev(dx=0, dy=0, dz=0, dc=0):
        xx, zz, cc = lax.rem(x + dx, 4), lax.rem(z + dz, 8), lax.rem(c + dc, 2)
        return (xx * 16 + zz * 2 + cc, lax.rem(y + dy, 4))

    sends = []

    def unit(i):
        k, d = i // 2, i % 2
        q = lax.rem(y + jnp.where(d == 0, 3 - k, 1 + k), 4)
        return q * 2 + d

    def a_copy(i):
        rows = pl.ds(pl.multiple_of(unit(i) * 256, 256), 256)
        return pltpu.make_async_copy(a_hbm.at[rows], a_v.at[rows], a_sem.at[i])

    barrier = pltpu.get_barrier_semaphore()
    xy = [(dx, dy) for dx in range(4) for dy in range(4) if dx + dy]
    peers = [dev(dy=1), dev(dy=3), dev(dc=1)] + [dev(dz=d) for d in range(1, 8)]
    peers += [dev(dx=dx, dy=dy) for dx, dy in xy if (dx, dy) not in ((0, 1), (0, 3))]
    for p in peers:
        pl.semaphore_signal(barrier, inc=1, device_id=p, device_id_type=MESH)
    s_copy = pltpu.make_async_copy(s_hbm, s_ref, a_sem.at[8])
    s_copy.start()
    a_copy(0).start()
    a_copy(1).start()
    s_copy.wait()

    def work(i, ahead=()):
        a_copy(i).wait()
        for j in ahead:
            a_copy(j).start()
        rows = pl.ds(pl.multiple_of(unit(i) * 256, 256), 256)
        v = lax.dot_general(
            s_ref[...], a_v[rows, :], (((1,), (1,)), ((), ())), preferred_element_type=F32
        )
        own[i // 2, i % 2] = v.reshape(NP, PR, 256)

    ydir = [dev(dy=1), dev(dy=3)]
    work(0, range(2, 4))
    work(1, range(4, 8))
    pl.semaphore_wait(barrier, len(peers))
    for p in range(NP):
        for d in range(2):
            sends.append(rc(own.at[0, d, p], rsr.at[d, 0, p], rs_s.at[d, 0, p], rs_r.at[d, 0, p], ydir[d]))
    arrivals = {(0, d, p): sends[2 * p + d] for p in range(NP) for d in range(2)}

    @pl.loop(2, 8)
    def _(i):
        work(i)

    def ag_send(p):
        for d in range(2):
            cp = rc(samp.at[y, p], samp.at[y, p], ag_s.at[d, p], ag_r.at[d, p], ydir[d])
            sends.append(cp)
            arrivals["ag", d, p] = cp

    def gram(p):
        v = None
        for d in range(2):
            u = lax.dot_general(
                samp[y, 0 : p + 1, d].reshape((p + 1) * PR, 256),
                samp[y, p, d],
                (((1,), (1,)), ((), ())),
                precision=HI,
                preferred_element_type=F32,
            )
            v = u if v is None else v + u
        n_ref[0 : (p + 1) * PR, p * PR : (p + 1) * PR] = v

    n_ref[...] = jnp.zeros_like(n_ref)
    for s in range(3):
        for p in range(NP):
            for d in range(2):
                arrivals[s, d, p].wait_recv()
                v = rsr[d, s, p] + own[s + 1, d, p]
                if s < 2:
                    rsr[d, s, p] = v
                    cp = rc(
                        rsr.at[d, s, p], rsr.at[d, s + 1, p], rs_s.at[d, s + 1, p], rs_r.at[d, s + 1, p], ydir[d]
                    )
                    sends.append(cp)
                    arrivals[s + 1, d, p] = cp
                else:
                    samp[y, p, d] = v
            if s == 2:
                if p < 3:
                    ag_send(p)
                gram(p)

    def ag_forward(p):
        for d in range(2):
            arrivals["ag", d, p].wait_recv()
            q = lax.rem(y + (3 if d == 0 else 1), 4)
            cp = rc(samp.at[q, p, d], samp.at[q, p, d], fw_s.at[d, p], fw_r.at[d, p], ydir[d])
            sends.append(cp)
            arrivals["fw", d, p] = cp

    def ag_end(p):
        for d in range(2):
            arrivals["fw", d, p].wait_recv()

    ring = (0, 1, 3, 2)

    def c_part(h, steps, first):
        a, b = GROUPS[h]
        r = 2 * SIZES[h]
        for i in steps:
            q = lax.rem(y + ring[i], 4)
            for d in range(2):
                hi, lo = split(samp[q, a:b, d].reshape(r, 256))
                shl[i, 0:r, 256 * d : 256 * d + 256] = hi
                shl[i, r : 2 * r, 256 * d : 256 * d + 256] = lo

        @pl.loop(0, 4)
        def _(j):
            cols = pl.ds(pl.multiple_of(512 * j, 512), 512)
            v = None
            for i in steps:
                rows = pl.ds(pl.multiple_of(512 * lax.rem(y + ring[i], 4), 512), 512)
                u = jnp.dot(shl[i, 0 : 2 * r], a_v[rows, cols], preferred_element_type=F32)
                v = u if v is None else v + u
            v = (v[0:r] + v[r : 2 * r]).reshape(2, r // 2, 512)
            ct[h][:, :, cols] = v if first else ct[h][:, :, cols] + v

    def c_send(h):
        cp = rc(ct[h].at[1 - c], crx[h], core_s.at[2 + h], core_r.at[2 + h], dev(dc=1))
        sends.append(cp)
        arrivals["c", h] = cp

    def c_work(h):
        c_part(h, range(4), True)
        c_send(h)

    def x_start(h):
        arrivals["c", h].wait_recv()
        for i in range(4):
            xs[h][i] = ct[h][c, :, 512 * i : 512 * i + 512] + crx[h][:, 512 * i : 512 * i + 512]
        arrivals["x", h] = [
            rc(xs[h].at[lax.rem(x + d, 4)], xrr[h].at[d - 1], px_s.at[h, d - 1], px_r.at[h, d - 1], dev(dx=d))
            for d in range(1, 4)
        ]
        sends.extend(arrivals["x", h])

    def z_start(h):
        for cp in arrivals["x", h]:
            cp.wait_recv()
        v = xs[h][x] + xrr[h][0] + xrr[h][1] + xrr[h][2]
        n = SIZES[h] // 2
        half = lax.broadcasted_iota(jnp.int32, (n, 128), 1) < 64
        for i in range(8):
            w = v[:, 128 * (i // 2) : 128 * (i // 2) + 128]
            top, bottom = w[0:n], w[n : 2 * n]
            if i % 2:
                zs[h][i] = jnp.where(half, pltpu.roll(top, 64, 1), bottom)
            else:
                zs[h][i] = jnp.where(half, top, pltpu.roll(bottom, 64, 1))
        arrivals["z", h] = [
            rc(zs[h].at[lax.rem(z + d, 8)], zr[h].at[d - 1], pz_s.at[h, d - 1], pz_r.at[h, d - 1], dev(dz=d))
            for d in range(1, 8)
        ]
        sends.extend(arrivals["z", h])

    def z_end(h):
        v = zs[h][z]
        for i, cp in enumerate(arrivals["z", h]):
            cp.wait_recv()
            v = v + zr[h][i]
        fin[h][c] = v
        cp = rc(fin[h].at[c], fin[h].at[c], core_s.at[4 + h], core_r.at[4 + h], dev(dc=1))
        sends.append(cp)
        arrivals["fin", h] = cp

    dot = functools.partial(jnp.dot, preferred_element_type=F32)

    def basis(first, last):
        whi, wlo = split(n_ref[:, 0:K])
        both = jnp.concatenate([whi[0:256, 0:256], wlo[0:256, 0:256]], axis=0)
        low = jnp.concatenate([whi[256:K], wlo[256:K]], axis=0)

        @pl.loop(first, last)
        def _(u):
            hi, lo = split(samp[u // 2, :, u % 2].reshape(K, 256))
            cols = pl.ds(pl.multiple_of(256 * u, 256), 256)
            v = dot(both, hi[0:256])
            bs[0:256, cols] = v[0:256] + (v[256:512] + dot(whi[0:256, 0:256], lo[0:256]))
            v = dot(low, hi)
            bs[256:K, cols] = v[0:64] + (v[64:128] + dot(whi[256:K], lo))

    def projected():
        for h in range(len(GROUPS)):
            arrivals["fin", h].wait_recv()
        rows = []
        for h in range(len(GROUPS)):
            for i in range(2):
                rows += [fin[h][i], pltpu.roll(fin[h][i], 64, 1)]
        v = jnp.dot(n_ref[:, 0:K], jnp.concatenate(rows, axis=0), precision=HI, preferred_element_type=F32)
        v = jnp.transpose(v)
        proj_out[...] = jnp.where(c == 0, v[0:32], v[32:64])

    low = lax.broadcasted_iota(jnp.int32, (B, 128), 1) < B

    def tile(i, j):
        return n_ref[B * i : B * i + B, 128 * j : 128 * j + 128]

    panels = [
        tile(0, 0),
        tile(0, 1),
        tile(1, 1),
        tile(2, 1),
        jnp.where(low, tile(0, 2), tile(1, 0)),
        jnp.where(low, tile(1, 2), tile(3, 1)),
        jnp.where(low, tile(2, 2), pltpu.roll(tile(3, 2), 64, 1)),
        tile(4, 2),
    ]
    for i, v in enumerate(panels):
        pk[i // 4, 4 * (i % 4) : 4 * (i % 4) + 4] = v.reshape(4, 16, 128)

    other = dev(dc=1)
    cp = rc(pk.at[1 - c], cr, core_s.at[0], core_r.at[0], other)
    sends.append(cp)
    cp.wait_recv()
    g1[...] = pk[c] + cr[...]
    me = 4 * x + y
    cps = []
    for i, (dx, dy) in enumerate(xy):
        to = 4 * lax.rem(x + dx, 4) + lax.rem(y + dy, 4)
        cps.append(rc(g1.at[to], xr.at[i], xy_s.at[i], xy_r.at[i], dev(dx=dx, dy=dy)))
    ag_forward(0)
    ag_send(3)
    v = g1[me]
    for i, cp in enumerate(cps):
        cp.wait_recv()
        v = v + xr[i]
    sends += cps
    zb[z] = v
    cps = [rc(zb.at[z], zb.at[z], z_s.at[d - 1], z_r.at[d - 1], dev(dz=d)) for d in range(1, 8)]
    ag_forward(1)
    ag_send(4)
    ag_forward(2)
    for cp in cps:
        cp.wait_recv()
    sends += cps
    v = zb[0]
    for i in range(1, 8):
        v = v + zb[i]
    gf[c, me] = v
    cps = [
        rc(gf.at[c, me], gf.at[c, me], xg_s.at[i], xg_r.at[i], dev(dx=dx, dy=dy)) for i, (dx, dy) in enumerate(xy)
    ]
    sends += cps
    ag_forward(3)
    ag_end(0)
    ag_end(1)
    ag_end(2)
    c_work(0)
    for cp in cps:
        cp.wait_recv()
    cp = rc(gf.at[c], gf.at[c], core_s.at[1], core_r.at[1], other)
    sends.append(cp)
    ag_forward(4)
    cp.wait_recv()

    def panel(i):
        return gf[i // 4, 4 * (i % 4) : 4 * (i % 4) + 4].reshape(B, 128)

    def put(i, j, v):
        n_ref[B * i : B * i + B, 128 * j : 128 * j + 128] = v

    put(0, 0, panel(0))
    put(0, 1, panel(1))
    put(1, 1, panel(2))
    put(2, 1, panel(3))
    v = panel(4)
    put(0, 2, jnp.where(low, v, 0.0))
    put(1, 0, jnp.where(low, 0.0, v))
    v = panel(5)
    put(1, 2, jnp.where(low, v, 0.0))
    put(3, 1, jnp.where(low, 0.0, v))
    v = panel(6)
    put(2, 2, jnp.where(low, v, 0.0))
    put(3, 2, jnp.where(low, pltpu.roll(v, 64, 1), 0.0))
    put(4, 2, panel(7))

    x_start(0)
    ag_end(3)
    ag_end(4)
    c_work(1)
    x_start(1)
    chol_step(0, n_ref)
    z_start(0)
    chol_step(1, n_ref)
    chol_step(2, n_ref)
    z_start(1)
    z_end(0)
    chol_step(3, n_ref)
    chol_step(4, n_ref)
    basis(0, 4)
    z_end(1)
    basis(4, 8)
    projected()
    for cp in sends:
        cp.wait_send()


def local(activations, sketch):
    dma = pltpu.SemaphoreType.DMA
    vm = pltpu.VMEM
    n = len(GROUPS)
    basis, proj = pl.pallas_call(
        main_kernel,
        out_shape=(vm((K, 2048), F32), vm((32, K), F32)),
        in_specs=[pl.BlockSpec(memory_space=pl.ANY)] * 2,
        out_specs=(pl.BlockSpec(memory_space=vm), pl.BlockSpec(memory_space=vm)),
        scratch_shapes=[
            vm((2048, 2048), BF),
            vm((K, 2048), BF),
            vm((4, 2, NP, PR, 256), F32),
            vm((2, 3, NP, PR, 256), F32),
            vm((4, NP, 2, PR, 256), F32),
            vm((K, 384), F32),
            vm((2, 16, 16, 128), F32),
            vm((16, 16, 128), F32),
            vm((16, 16, 128), F32),
            vm((15, 16, 128), F32),
            vm((8, 16, 128), F32),
            vm((2, 16, 16, 128), F32),
            vm((4, 4 * max(SIZES), 512), BF),
            *[vm((2, r, 2048), F32) for r in SIZES],
            *[vm((r, 2048), F32) for r in SIZES],
            *[vm((4, r, 512), F32) for r in SIZES],
            *[vm((3, r, 512), F32) for r in SIZES],
            *[vm((8, r // 2, 128), F32) for r in SIZES],
            *[vm((7, r // 2, 128), F32) for r in SIZES],
            *[vm((2, r // 2, 128), F32) for r in SIZES],
            dma((9,)),
            dma((2, 3, NP)),
            dma((2, 3, NP)),
            dma((2, NP)),
            dma((2, NP)),
            dma((2, NP)),
            dma((2, NP)),
            dma((2 + 2 * n,)),
            dma((2 + 2 * n,)),
            dma((15,)),
            dma((15,)),
            dma((7,)),
            dma((7,)),
            dma((15,)),
            dma((15,)),
            dma((n, 3)),
            dma((n, 3)),
            dma((n, 7)),
            dma((n, 7)),
        ],
        compiler_params=pltpu.CompilerParams(
            collective_id=0, has_side_effects=True, vmem_limit_bytes=58 * 1024 * 1024
        ),
        name="main",
    )(activations, sketch.T)
    return basis.T, proj


def solution(mesh):
    in_specs = (P("tok", "hid"), P("hid", None))
    out_specs = (P("tok", None), P(("hid", "tok"), None))
    return jax.shard_map(local, mesh=mesh, in_specs=in_specs, out_specs=out_specs, check_vma=False)
```

```python
import functools

import jax
import jax.numpy as jnp
from jax import lax
from jax.experimental import pallas as pl
from jax.experimental.pallas import tpu as pltpu
from jax.sharding import PartitionSpec as P

MESH = pl.DeviceIdType.MESH
HI = lax.Precision.HIGHEST
F32 = jnp.float32
BF = jnp.bfloat16
K = 320
B = 64
NP = 5
PR = K // NP
GROUPS = ((0, 2), (2, 4), (4, 5))
SIZES = tuple((b - a) * PR // 2 for a, b in GROUPS)


def rc(src, dst, ssem, rsem, dev):
    cp = pltpu.make_async_remote_copy(
        src_ref=src, dst_ref=dst, send_sem=ssem, recv_sem=rsem, device_id=dev, device_id_type=MESH
    )
    cp.start()
    return cp


def split(v):
    hi = v.astype(BF)
    return hi, (v - hi.astype(F32)).astype(BF)


def factor(aug):
    subl = lax.broadcasted_iota(jnp.int32, (8, 128), 0)
    w = 16
    n = w // 8

    def spread(v, i):
        return jnp.broadcast_to(v[i : i + 1, :], (8, 128))

    parts = [aug[8 * i : 8 * i + 8, :] for i in range(8)]
    for g in range(0, 8, n):
        cur = parts[g:]
        cols = [[jnp.broadcast_to(v[:, 8 * g + j : 8 * g + j + 1], (8, 128)) for j in range(w)] for v in cur]
        scale = [jnp.zeros((8, 128), F32) for _ in range(n)]
        for t in range(w):
            o, i = t // 8, t % 8
            piv = spread(cols[o][t], i)
            inv = 1.0 / piv
            scale[o] = jnp.where(subl == i, lax.rsqrt(piv), scale[o])
            row = spread(cur[o], i)
            later = {j: spread(cols[o][j], i) for j in range(t + 1, w)}
            for h in range(o, len(cur)):
                f = cols[h][t] * inv
                if h == o:
                    f = jnp.where(subl > i, f, 0.0)
                for j in range(t + 1, w):
                    cols[h][j] = cols[h][j] - f * later[j]
                cur[h] = cur[h] - f * row
        parts = parts[:g] + [cur[o] * scale[o] for o in range(n)] + cur[n:]
    return jnp.concatenate(parts, axis=0)


def chol_step(J, n_ref):
    r0 = B * J
    tile = 128 * (J // 2)
    blk = n_ref[r0 : r0 + B, tile : tile + 128]
    if J % 2:
        blk = pltpu.roll(blk, 64, 1)
    lanes = lax.broadcasted_iota(jnp.int32, (B, 128), 1)
    rows = lax.broadcasted_iota(jnp.int32, (B, 128), 0)
    w = pltpu.roll(factor(jnp.where(lanes < B, blk, (lanes - B == rows).astype(F32))), 64, 1)[:, :B]
    col = lax.broadcasted_iota(jnp.int32, (B, 384), 1)
    row = lax.broadcasted_iota(jnp.int32, (B, 384), 0)
    here = (col >= r0) & (col < r0 + B)
    rin = jnp.where(here, (row + r0 == col).astype(F32), n_ref[r0 : r0 + B, :])
    r = jnp.dot(w, rin, precision=HI, preferred_element_type=F32)
    n_ref[r0 : r0 + B, :] = jnp.where(col < r0 + B, r, 0.0)
    if J < K // B - 1:
        m = K - r0 - B
        upd = lax.dot_general(r, r, (((0,), (0,)), ((), ())), precision=HI, preferred_element_type=F32)
        colb = lax.broadcasted_iota(jnp.int32, (m, 384), 1)
        old = jnp.where((colb >= r0) & (colb < r0 + B), 0.0, n_ref[r0 + B : K, :])
        n_ref[r0 + B : K, :] = old - upd[r0 + B : K, :]


def main_kernel(
    a_hbm, s_hbm, bs, proj_out,
    a_v, s_ref, own, rsr, samp, n_ref, pk, cr, g1, xr, zb, gf, shl,
    ct0, ct1, ct2, crx0, crx1, crx2, xs0, xs1, xs2, xrr0, xrr1, xrr2, zs0, zs1, zs2, zr0, zr1, zr2,
    fin0, fin1, fin2,
    a_sem, rs_s, rs_r, ag_s, ag_r, fw_s, fw_r, core_s, core_r, xy_s, xy_r, z_s, z_r, xg_s, xg_r,
    px_s, px_r, pz_s, pz_r,
):
    ct, crx, xs, xrr = (ct0, ct1, ct2), (crx0, crx1, crx2), (xs0, xs1, xs2), (xrr0, xrr1, xrr2)
    zs, zr, fin = (zs0, zs1, zs2), (zr0, zr1, zr2), (fin0, fin1, fin2)
    t = lax.axis_index("tok")
    y = lax.axis_index("hid")
    x, z, c = t // 16, (t // 2) % 8, t % 2

    def dev(dx=0, dy=0, dz=0, dc=0):
        xx, zz, cc = lax.rem(x + dx, 4), lax.rem(z + dz, 8), lax.rem(c + dc, 2)
        return (xx * 16 + zz * 2 + cc, lax.rem(y + dy, 4))

    sends = []

    def unit(i):
        k, d = i // 2, i % 2
        q = lax.rem(y + jnp.where(d == 0, 3 - k, 1 + k), 4)
        return q * 2 + d

    def a_copy(i):
        rows = pl.ds(pl.multiple_of(unit(i) * 256, 256), 256)
        return pltpu.make_async_copy(a_hbm.at[rows], a_v.at[rows], a_sem.at[i])

    barrier = pltpu.get_barrier_semaphore()
    xy = [(dx, dy) for dx in range(4) for dy in range(4) if dx + dy]
    peers = [dev(dy=1), dev(dy=3), dev(dc=1)] + [dev(dz=d) for d in range(1, 8)]
    peers += [dev(dx=dx, dy=dy) for dx, dy in xy if (dx, dy) not in ((0, 1), (0, 3))]
    for p in peers:
        pl.semaphore_signal(barrier, inc=1, device_id=p, device_id_type=MESH)
    s_copy = pltpu.make_async_copy(s_hbm, s_ref, a_sem.at[8])
    s_copy.start()
    a_copy(0).start()
    a_copy(1).start()
    s_copy.wait()

    def work(i, ahead=()):
        a_copy(i).wait()
        for j in ahead:
            a_copy(j).start()
        rows = pl.ds(pl.multiple_of(unit(i) * 256, 256), 256)
        v = lax.dot_general(
            s_ref[...], a_v[rows, :], (((1,), (1,)), ((), ())), preferred_element_type=F32
        )
        own[i // 2, i % 2] = v.reshape(NP, PR, 256)

    ydir = [dev(dy=1), dev(dy=3)]
    work(0, range(2, 4))
    work(1, range(4, 8))
    pl.semaphore_wait(barrier, len(peers))
    for p in range(NP):
        for d in range(2):
            sends.append(rc(own.at[0, d, p], rsr.at[d, 0, p], rs_s.at[d, 0, p], rs_r.at[d, 0, p], ydir[d]))
    arrivals = {(0, d, p): sends[2 * p + d] for p in range(NP) for d in range(2)}

    @pl.loop(2, 8)
    def _(i):
        work(i)

    def ag_send(p):
        for d in range(2):
            cp = rc(samp.at[y, p], samp.at[y, p], ag_s.at[d, p], ag_r.at[d, p], ydir[d])
            sends.append(cp)
            arrivals["ag", d, p] = cp

    def gram(p):
        v = None
        for d in range(2):
            u = lax.dot_general(
                samp[y, 0 : p + 1, d].reshape((p + 1) * PR, 256),
                samp[y, p, d],
                (((1,), (1,)), ((), ())),
                precision=HI,
                preferred_element_type=F32,
            )
            v = u if v is None else v + u
        n_ref[0 : (p + 1) * PR, p * PR : (p + 1) * PR] = v

    n_ref[...] = jnp.zeros_like(n_ref)
    for s in range(3):
        for p in range(NP):
            for d in range(2):
                arrivals[s, d, p].wait_recv()
                v = rsr[d, s, p] + own[s + 1, d, p]
                if s < 2:
                    rsr[d, s, p] = v
                    cp = rc(
                        rsr.at[d, s, p], rsr.at[d, s + 1, p], rs_s.at[d, s + 1, p], rs_r.at[d, s + 1, p], ydir[d]
                    )
                    sends.append(cp)
                    arrivals[s + 1, d, p] = cp
                else:
                    samp[y, p, d] = v
            if s == 2:
                ag_send(p)
                gram(p)

    def ag_forward(p):
        for d in range(2):
            arrivals["ag", d, p].wait_recv()
            q = lax.rem(y + (3 if d == 0 else 1), 4)
            cp = rc(samp.at[q, p, d], samp.at[q, p, d], fw_s.at[d, p], fw_r.at[d, p], ydir[d])
            sends.append(cp)
            arrivals["fw", d, p] = cp

    def ag_end(p):
        for d in range(2):
            arrivals["fw", d, p].wait_recv()

    ring = (0, 1, 3, 2)

    def c_part(h, steps, first):
        a, b = GROUPS[h]
        r = 2 * SIZES[h]
        for i in steps:
            q = lax.rem(y + ring[i], 4)
            for d in range(2):
                hi, lo = split(samp[q, a:b, d].reshape(r, 256))
                shl[i, 0:r, 256 * d : 256 * d + 256] = hi
                shl[i, r : 2 * r, 256 * d : 256 * d + 256] = lo

        @pl.loop(0, 4)
        def _(j):
            cols = pl.ds(pl.multiple_of(512 * j, 512), 512)
            v = None
            for i in steps:
                rows = pl.ds(pl.multiple_of(512 * lax.rem(y + ring[i], 4), 512), 512)
                u = jnp.dot(shl[i, 0 : 2 * r], a_v[rows, cols], preferred_element_type=F32)
                v = u if v is None else v + u
            v = (v[0:r] + v[r : 2 * r]).reshape(2, r // 2, 512)
            ct[h][:, :, cols] = v if first else ct[h][:, :, cols] + v

    def c_send(h):
        cp = rc(ct[h].at[1 - c], crx[h], core_s.at[2 + h], core_r.at[2 + h], dev(dc=1))
        sends.append(cp)
        arrivals["c", h] = cp

    def c_work(h):
        c_part(h, range(4), True)
        c_send(h)

    def x_start(h):
        arrivals["c", h].wait_recv()
        for i in range(4):
            xs[h][i] = ct[h][c, :, 512 * i : 512 * i + 512] + crx[h][:, 512 * i : 512 * i + 512]
        arrivals["x", h] = [
            rc(xs[h].at[lax.rem(x + d, 4)], xrr[h].at[d - 1], px_s.at[h, d - 1], px_r.at[h, d - 1], dev(dx=d))
            for d in range(1, 4)
        ]
        sends.extend(arrivals["x", h])

    def z_start(h):
        for cp in arrivals["x", h]:
            cp.wait_recv()
        v = xs[h][x] + xrr[h][0] + xrr[h][1] + xrr[h][2]
        n = SIZES[h] // 2
        half = lax.broadcasted_iota(jnp.int32, (n, 128), 1) < 64
        for i in range(8):
            w = v[:, 128 * (i // 2) : 128 * (i // 2) + 128]
            top, bottom = w[0:n], w[n : 2 * n]
            if i % 2:
                zs[h][i] = jnp.where(half, pltpu.roll(top, 64, 1), bottom)
            else:
                zs[h][i] = jnp.where(half, top, pltpu.roll(bottom, 64, 1))
        arrivals["z", h] = [
            rc(zs[h].at[lax.rem(z + d, 8)], zr[h].at[d - 1], pz_s.at[h, d - 1], pz_r.at[h, d - 1], dev(dz=d))
            for d in range(1, 8)
        ]
        sends.extend(arrivals["z", h])

    def z_end(h):
        v = zs[h][z]
        for i, cp in enumerate(arrivals["z", h]):
            cp.wait_recv()
            v = v + zr[h][i]
        fin[h][c] = v
        cp = rc(fin[h].at[c], fin[h].at[c], core_s.at[5 + h], core_r.at[5 + h], dev(dc=1))
        sends.append(cp)
        arrivals["fin", h] = cp

    dot = functools.partial(jnp.dot, preferred_element_type=F32)

    def basis(first, last):
        whi, wlo = split(n_ref[:, 0:K])
        both = jnp.concatenate([whi[0:256, 0:256], wlo[0:256, 0:256]], axis=0)
        low = jnp.concatenate([whi[256:K], wlo[256:K]], axis=0)

        @pl.loop(first, last)
        def _(u):
            hi, lo = split(samp[u // 2, :, u % 2].reshape(K, 256))
            cols = pl.ds(pl.multiple_of(256 * u, 256), 256)
            v = dot(both, hi[0:256])
            bs[0:256, cols] = v[0:256] + (v[256:512] + dot(whi[0:256, 0:256], lo[0:256]))
            v = dot(low, hi)
            bs[256:K, cols] = v[0:64] + (v[64:128] + dot(whi[256:K], lo))

    def projected():
        for h in range(len(GROUPS)):
            arrivals["fin", h].wait_recv()
        rows = []
        for h in range(len(GROUPS)):
            for i in range(2):
                rows += [fin[h][i], pltpu.roll(fin[h][i], 64, 1)]
        v = jnp.dot(n_ref[:, 0:K], jnp.concatenate(rows, axis=0), precision=HI, preferred_element_type=F32)
        v = jnp.transpose(v)
        proj_out[...] = jnp.where(c == 0, v[0:32], v[32:64])

    low = lax.broadcasted_iota(jnp.int32, (B, 128), 1) < B

    def tile(i, j):
        return n_ref[B * i : B * i + B, 128 * j : 128 * j + 128]

    panels = [
        tile(0, 0),
        tile(0, 1),
        tile(1, 1),
        tile(2, 1),
        jnp.where(low, tile(0, 2), tile(1, 0)),
        jnp.where(low, tile(1, 2), tile(3, 1)),
        jnp.where(low, tile(2, 2), pltpu.roll(tile(3, 2), 64, 1)),
        tile(4, 2),
    ]
    for i, v in enumerate(panels):
        pk[i // 4, 4 * (i % 4) : 4 * (i % 4) + 4] = v.reshape(4, 16, 128)

    other = dev(dc=1)
    cp = rc(pk.at[1 - c], cr, core_s.at[0], core_r.at[0], other)
    sends.append(cp)
    cp.wait_recv()
    g1[...] = pk[c] + cr[...]
    me = 4 * x + y
    cps = []
    for i, (dx, dy) in enumerate(xy):
        to = 4 * lax.rem(x + dx, 4) + lax.rem(y + dy, 4)
        cps.append(rc(g1.at[to], xr.at[i], xy_s.at[i], xy_r.at[i], dev(dx=dx, dy=dy)))
    ag_forward(0)
    v = g1[me]
    for i, cp in enumerate(cps):
        cp.wait_recv()
        v = v + xr[i]
    sends += cps
    zb[z] = v
    cps = [rc(zb.at[z], zb.at[z], z_s.at[d - 1], z_r.at[d - 1], dev(dz=d)) for d in range(1, 8)]
    ag_forward(1)
    for cp in cps:
        cp.wait_recv()
    sends += cps
    v = zb[0]
    for i in range(1, 8):
        v = v + zb[i]
    gf[c, me] = v
    cps = [
        rc(gf.at[c, me], gf.at[c, me], xg_s.at[i], xg_r.at[i], dev(dx=dx, dy=dy)) for i, (dx, dy) in enumerate(xy)
    ]
    sends += cps
    ag_forward(2)
    c_part(0, (0, 1, 2), True)
    ag_forward(3)
    for cp in cps:
        cp.wait_recv()
    cp = rc(gf.at[c], gf.at[c], core_s.at[1], core_r.at[1], other)
    sends.append(cp)
    ag_forward(4)
    cp.wait_recv()

    def panel(i):
        return gf[i // 4, 4 * (i % 4) : 4 * (i % 4) + 4].reshape(B, 128)

    def put(i, j, v):
        n_ref[B * i : B * i + B, 128 * j : 128 * j + 128] = v

    put(0, 0, panel(0))
    put(0, 1, panel(1))
    put(1, 1, panel(2))
    put(2, 1, panel(3))
    v = panel(4)
    put(0, 2, jnp.where(low, v, 0.0))
    put(1, 0, jnp.where(low, 0.0, v))
    v = panel(5)
    put(1, 2, jnp.where(low, v, 0.0))
    put(3, 1, jnp.where(low, 0.0, v))
    v = panel(6)
    put(2, 2, jnp.where(low, v, 0.0))
    put(3, 2, jnp.where(low, pltpu.roll(v, 64, 1), 0.0))
    put(4, 2, panel(7))

    ag_end(0)
    ag_end(1)
    c_part(0, (3,), False)
    c_send(0)
    ag_end(2)
    ag_end(3)
    c_work(1)
    x_start(0)
    ag_end(4)
    c_work(2)
    x_start(1)
    chol_step(0, n_ref)
    x_start(2)
    z_start(0)
    chol_step(1, n_ref)
    chol_step(2, n_ref)
    z_start(1)
    z_end(0)
    chol_step(3, n_ref)
    z_start(2)
    chol_step(4, n_ref)
    basis(0, 4)
    z_end(1)
    basis(4, 7)
    z_end(2)
    basis(7, 8)
    projected()
    for cp in sends:
        cp.wait_send()


def local(activations, sketch):
    dma = pltpu.SemaphoreType.DMA
    vm = pltpu.VMEM
    n = len(GROUPS)
    basis, proj = pl.pallas_call(
        main_kernel,
        out_shape=(vm((K, 2048), F32), vm((32, K), F32)),
        in_specs=[pl.BlockSpec(memory_space=pl.ANY)] * 2,
        out_specs=(pl.BlockSpec(memory_space=vm), pl.BlockSpec(memory_space=vm)),
        scratch_shapes=[
            vm((2048, 2048), BF),
            vm((K, 2048), BF),
            vm((4, 2, NP, PR, 256), F32),
            vm((2, 3, NP, PR, 256), F32),
            vm((4, NP, 2, PR, 256), F32),
            vm((K, 384), F32),
            vm((2, 16, 16, 128), F32),
            vm((16, 16, 128), F32),
            vm((16, 16, 128), F32),
            vm((15, 16, 128), F32),
            vm((8, 16, 128), F32),
            vm((2, 16, 16, 128), F32),
            vm((4, 4 * max(SIZES), 512), BF),
            *[vm((2, r, 2048), F32) for r in SIZES],
            *[vm((r, 2048), F32) for r in SIZES],
            *[vm((4, r, 512), F32) for r in SIZES],
            *[vm((3, r, 512), F32) for r in SIZES],
            *[vm((8, r // 2, 128), F32) for r in SIZES],
            *[vm((7, r // 2, 128), F32) for r in SIZES],
            *[vm((2, r // 2, 128), F32) for r in SIZES],
            dma((9,)),
            dma((2, 3, NP)),
            dma((2, 3, NP)),
            dma((2, NP)),
            dma((2, NP)),
            dma((2, NP)),
            dma((2, NP)),
            dma((2 + 2 * n,)),
            dma((2 + 2 * n,)),
            dma((15,)),
            dma((15,)),
            dma((7,)),
            dma((7,)),
            dma((15,)),
            dma((15,)),
            dma((n, 3)),
            dma((n, 3)),
            dma((n, 7)),
            dma((n, 7)),
        ],
        compiler_params=pltpu.CompilerParams(
            collective_id=0, has_side_effects=True, vmem_limit_bytes=58 * 1024 * 1024
        ),
        name="main",
    )(activations, sketch.T)
    return basis.T, proj


def solution(mesh):
    in_specs = (P("tok", "hid"), P("hid", None))
    out_specs = (P("tok", None), P(("hid", "tok"), None))
    return jax.shard_map(local, mesh=mesh, in_specs=in_specs, out_specs=out_specs, check_vma=False)
```
